256 devices in a mesh: seq: 64 (over y, z_lo, x), chan: 4 (over z_hi, core).
Axes of the slice: x: 4, y: 4, z: 8 (z_hi: 2, z_lo: 4; z = z_hi * 4 + z_lo), core: 2. Of those that a mesh axis runs over, the one named last changes fastest.
Arguments:
- query_input: bfloat16 [16384, 4096], P('seq', 'chan'), may hold values from -6 to 6
- key_input: bfloat16 [16384, 4096], P('seq', 'chan'), may hold values from -6 to 6
- value_input: bfloat16 [16384, 4096], P('seq', 'chan'), may hold values from -6 to 6
- spectra: float32 [2, 128, 256, 4096], P(None, 'seq', None, 'chan'), may hold values from -4 to 4
- skip_gain: float32 [4096], P('chan'), may hold values from 0.5 to 1.5
- proj_weight: bfloat16 [4096, 4096], P(('chan', 'seq')), may hold values from -0.09375 to 0.09375
Outputs:
- mixed: bfloat16 [16384, 4096], P('seq', 'chan')
The draws below stay inside these ranges and needn't reach their ends.
All inputs are finite; a program needn't handle non-finite values.
Results may differ from the reference program's by a relative error of at most 0.0049.
Values may be sent and summed in bfloat16 or wider, within the bound.
No kernel may reach another device: no remote copies, remote signals or barrier semaphores. Data moves between devices by JAX's collectives and lax.ppermute only.
A program may use at most 128 MiB of HBM per device.

```python
import jax
import jax.numpy as jnp
from jax import lax

CH = 4096
DOUT = 4096
TOK_DEV = 256
SEQ_LEN = 16384
BLOCKS = 128


def steps_of(key, shape, shards, smallest, largest):
    gain, own = 1.0, jax.random.fold_in(key, 6)
    for position, blocks in shards:
        heights = jnp.exp(jax.random.uniform(jax.random.fold_in(own, position), (blocks,), jnp.float32, smallest / len(shards), largest / len(shards)))
        gain = gain * jnp.repeat(heights, shape[position] // blocks).reshape([-1 if axis == position else 1 for axis in range(len(shape))])
    return gain


def noise(own_key, shape, deviation, limit, cuts=(), kind=jnp.bfloat16):
    drawn = deviation * jax.random.normal(own_key, shape, jnp.float32)
    if cuts:
        drawn = drawn * steps_of(own_key, shape, cuts, -0.22, 0.18)
    return jnp.clip(drawn, -limit, limit).astype(kind)


def setup_inputs(seed: int = 0) -> dict:
    arg_keys = jax.random.split(jax.random.key(seed), 7)
    return {
        "query_input": noise(arg_keys[0], (SEQ_LEN, CH), 1.0, 6.0, ((0, 64), (1, 4))),
        "key_input": noise(arg_keys[1], (SEQ_LEN, CH), 1.0, 6.0, ((0, 64), (1, 4))),
        "value_input": noise(arg_keys[2], (SEQ_LEN, CH), 1.0, 6.0, ((0, 64), (1, 4))),
        "spectra": noise(arg_keys[3], (2, BLOCKS, TOK_DEV, CH), 0.7, 4.0, ((1, 64), (3, 4)), jnp.float32),
        "skip_gain": jnp.clip(0.5 + 1.0 * jax.random.uniform(arg_keys[4], (CH,), jnp.float32) ** steps_of(arg_keys[4], (CH,), ((0, 4),), -0.2, 0.2), 0.5, 1.5),
        "proj_weight": noise(arg_keys[5], (DOUT, CH), CH ** -0.5, 0.09375, ((0, 256),)),
    }


def reference(query_input, key_input, value_input, spectra, skip_gain, proj_weight):
    conv_input = key_input.astype(jnp.float32) * value_input.astype(jnp.float32)
    seq_len = conv_input.shape[0]
    full_len = 2 * seq_len
    group_width = min(CH, 256)
    group_count = CH // group_width

    def filter_group(block_index):
        col_start = block_index * group_width
        columns = lax.dynamic_slice_in_dim(conv_input, col_start, group_width, 1)
        spec_real = lax.dynamic_slice_in_dim(spectra[0], col_start, group_width, 2)
        spec_imag = lax.dynamic_slice_in_dim(spectra[1], col_start, group_width, 2)
        response = (spec_real + 1j * spec_imag).transpose(1, 0, 2).reshape(full_len, group_width)
        frequency = jnp.fft.fft(columns, n=full_len, axis=0)
        inverse = jnp.fft.ifft(frequency * response, axis=0)
        return jnp.real(inverse)[:seq_len].astype(jnp.float32)

    grouped = lax.map(filter_group, jnp.arange(group_count, dtype=jnp.int32))
    filtered = grouped.transpose(1, 0, 2).reshape(seq_len, CH)
    gated = (query_input.astype(jnp.float32) * (filtered + skip_gain[None, :] * conv_input)).astype(jnp.bfloat16)
    mixed = jnp.dot(gated, proj_weight.T, preferred_element_type=jnp.float32)
    return mixed.astype(jnp.bfloat16)
```

```python
import numpy as np

import jax
import jax.numpy as jnp
import ml_dtypes
from jax import lax
from jax.experimental import pallas as pl
from jax.experimental.pallas import tpu as pltpu
from jax.sharding import Mesh, PartitionSpec as P

BF, F32 = jnp.bfloat16, jnp.float32
SEQ = ("y", "z", "x")
TOK, NSEQ, CLASSES = 256, 64, 128
FULL = CLASSES * TOK


def split(table):
    hi = table.astype(ml_dtypes.bfloat16)
    lo = (table - hi.astype(np.float64)).astype(ml_dtypes.bfloat16)
    return hi, lo


def tables():
    classes = np.concatenate([np.arange(0, CLASSES, 2), np.arange(1, CLASSES, 2)])
    blocks, rows = np.arange(NSEQ), np.arange(TOK)
    turn = 2 * np.pi * (classes[:, None] * blocks[None, :] % CLASSES) / CLASSES
    fwd_hi, fwd_lo = split(np.concatenate([np.cos(turn), -np.sin(turn)], 0))
    first = np.concatenate([fwd_hi, fwd_lo], 1)
    inv = np.concatenate([np.cos(turn.T), -np.sin(turn.T)], 1) / FULL
    last = np.concatenate(split(inv), 0)
    turn = 2 * np.pi * (rows[:, None] * rows[None, :] % TOK) / TOK
    row_hi, row_lo = split(np.concatenate([np.cos(turn), np.sin(turn)], 0))
    turn = 2 * np.pi * (classes[:, None] * rows[None, :]) / FULL
    return first, last, row_hi, row_lo, np.cos(turn).astype(np.float32), np.sin(turn).astype(np.float32)


def dot(a, b):
    return lax.dot_general(a, b, (((1,), (0,)), ((), ())), preferred_element_type=F32)


def parts(value):
    hi = value.astype(BF)
    return hi, (value - hi.astype(F32)).astype(BF)


def prep_kernel(k_ref, v_ref, s_ref, o_ref):
    conv = k_ref[...].astype(F32) * v_ref[...].astype(F32)
    o_ref[:, :TOK] = conv.T.astype(BF)
    for j in range(4):
        o_ref[:, TOK * (j + 1) : TOK * (j + 2)] = s_ref[j].T.astype(BF)


def prep(key, value, spectra):
    width = key.shape[1]
    blk = 128
    return pl.pallas_call(
        prep_kernel,
        grid=(width // blk,),
        in_specs=[
            pl.BlockSpec((TOK, blk), lambda i: (0, i)),
            pl.BlockSpec((TOK, blk), lambda i: (0, i)),
            pl.BlockSpec((4, TOK, blk), lambda i: (0, 0, i)),
        ],
        out_specs=pl.BlockSpec((blk, 5 * TOK), lambda i: (i, 0)),
        out_shape=jax.ShapeDtypeStruct((width, 5 * TOK), BF),
        compiler_params=pltpu.CompilerParams(vmem_limit_bytes=32 << 20),
        name="prep",
    )(key, value, spectra)


GROUP = 2


def fft_kernel(r_ref, first_ref, last_ref, hi_ref, lo_ref, tc_ref, ts_ref, o_ref, xs, ys):
    chans = r_ref.shape[0] // NSEQ

    def widen(i, _):
        rows = pl.ds(pl.multiple_of(i * 64, 64), 64)
        for c in range(10):
            xs[c, rows, :] = r_ref[rows, c * 128 : c * 128 + 128].astype(F32)
        return 0

    lax.fori_loop(0, r_ref.shape[0] // 64, widen, 0)
    first, last = first_ref[...], last_ref[...]
    hi_table, lo_table = hi_ref[...], lo_ref[...]
    tc, ts = tc_ref[...], ts_ref[...]

    def rows_of(h, col):
        rows = pl.ds(h, NSEQ, stride=chans)
        return jnp.concatenate([xs[2 * col, rows, :], xs[2 * col + 1, rows, :]], 1)

    def row_section(stacked):
        hi, lo = parts(stacked)
        return dot(hi, hi_table) + dot(lo, hi_table) + dot(hi, lo_table)

    def step(g, _):
        stacked = []
        for j in range(GROUP):
            x = rows_of(g * GROUP + j, 0).astype(BF)
            a = dot(first, jnp.concatenate([x, x], 0))
            ar, ai = a[:CLASSES], a[CLASSES:]
            ar, ai = ar * tc + ai * ts, ai * tc - ar * ts
            stacked += [jnp.concatenate([ar, ai], 1), jnp.concatenate([ai, -ar], 1)]
        freq = row_section(jnp.concatenate(stacked, 0))
        stacked = []
        for j in range(GROUP):
            h = g * GROUP + j
            rr = jnp.concatenate([rows_of(h, 1), rows_of(h, 2)], 0)
            ri = jnp.concatenate([rows_of(h, 3), rows_of(h, 4)], 0)
            base = 2 * CLASSES * j
            xr, xi = freq[base : base + CLASSES], freq[base + CLASSES : base + 2 * CLASSES]
            pr, pi = rr * xr - ri * xi, rr * xi + ri * xr
            stacked += [jnp.concatenate([pr, -pi], 1), jnp.concatenate([pi, pr], 1)]
        back = row_section(jnp.concatenate(stacked, 0))
        for j in range(GROUP):
            h = g * GROUP + j
            base = 2 * CLASSES * j
            br, bi = back[base : base + CLASSES], back[base + CLASSES : base + 2 * CLASSES]
            br, bi = br * tc - bi * ts, bi * tc + br * ts
            hi, lo = parts(jnp.concatenate([br, bi], 0))
            both = dot(last, hi)
            y = both[:NSEQ] + both[NSEQ:] + dot(last[:NSEQ], lo)
            for c in range(2):
                ys[c, pl.ds(h, NSEQ, stride=chans), :] = y[:, c * 128 : c * 128 + 128]
        return 0

    lax.fori_loop(0, chans // GROUP, step, 0)
    for c in range(2):
        o_ref[:, c * 128 : c * 128 + 128] = ys[c].astype(BF)


def convolve(received):
    rows = received.shape[0]
    consts = [jnp.asarray(t) for t in tables()]
    return pl.pallas_call(
        fft_kernel,
        in_specs=[pl.BlockSpec(memory_space=pltpu.VMEM)] * 7,
        out_specs=pl.BlockSpec(memory_space=pltpu.VMEM),
        out_shape=jax.ShapeDtypeStruct((rows, TOK), BF),
        scratch_shapes=[pltpu.VMEM((10, rows, 128), F32), pltpu.VMEM((2, rows, 128), F32)],
        compiler_params=pltpu.CompilerParams(vmem_limit_bytes=40 << 20),
        name="convolve",
    )(received, *consts)


def gate_kernel(y_ref, q_ref, k_ref, v_ref, s_ref, o_ref):
    conv = k_ref[...].astype(F32) * v_ref[...].astype(F32)
    filtered = y_ref[...].astype(F32).T
    o_ref[...] = (q_ref[...].astype(F32) * (filtered + s_ref[...] * conv)).astype(BF)


def gate(y, query, key, value, gain):
    width = key.shape[1]
    blk = 128
    tok = pl.BlockSpec((TOK, blk), lambda i: (0, i))
    return pl.pallas_call(
        gate_kernel,
        grid=(width // blk,),
        in_specs=[pl.BlockSpec((blk, TOK), lambda i: (i, 0)), tok, tok, tok, pl.BlockSpec((1, blk), lambda i: (0, i))],
        out_specs=tok,
        out_shape=jax.ShapeDtypeStruct((TOK, width), BF),
        compiler_params=pltpu.CompilerParams(vmem_limit_bytes=32 << 20),
        name="gate",
    )(y, query, key, value, gain)


def project_kernel(order_ref, g0, g1, g2, g3, w_ref, o_ref, acc):
    i = pl.program_id(0)
    for j, g_ref in enumerate((g0, g1, g2, g3)):

        @pl.when(i == j)
        def _():
            g = g_ref[...]
            for y in range(4):
                w = jnp.concatenate([w_ref[y, x, z] for z in range(4) for x in range(4)], 0)
                cols = slice(y * 256, y * 256 + 256)
                term = lax.dot_general(g, w, (((1,), (1,)), ((), ())), preferred_element_type=F32)
                total = term if j == 0 else acc[:, cols] + term
                if j == 3:
                    o_ref[:, cols] = total.astype(BF)
                else:
                    acc[:, cols] = total


def project(order, pieces, weight):
    width = pieces[0].shape[1]
    outs = weight.shape[0] * weight.shape[1] * weight.shape[2] * weight.shape[3]
    whole = pl.BlockSpec((TOK, width), lambda i, order: (0, 0))
    return pl.pallas_call(
        project_kernel,
        grid_spec=pltpu.PrefetchScalarGridSpec(
            num_scalar_prefetch=1,
            grid=(4,),
            in_specs=[whole] * 4
            + [pl.BlockSpec(weight.shape[:4] + (width,), lambda i, order: (0, 0, 0, 0, order[i]))],
            out_specs=pl.BlockSpec((TOK, outs), lambda i, order: (0, 0)),
            scratch_shapes=[pltpu.VMEM((TOK, outs), F32)],
        ),
        out_shape=jax.ShapeDtypeStruct((TOK, outs), BF),
        compiler_params=pltpu.CompilerParams(vmem_limit_bytes=32 << 20),
        name="project",
    )(order, *pieces, weight)


def gather_weight(weight):
    z = lax.axis_index("z")
    from_z = [weight] + [
        lax.ppermute(weight, "z", [(a, (a + d) % 4) for a in range(4)]) for d in (1, 2, 3)
    ]
    stacked = jnp.stack(from_z)
    ordered = jnp.stack([lax.dynamic_index_in_dim(stacked, (z - a) % 4, 0, False) for a in range(4)])
    return lax.all_gather(ordered[None], ("y", "x"), axis=0, tiled=True).reshape(
        (4, 4, 4) + weight.shape
    )


def local(query, key, value, spectra, gain, weight):
    swap = [(0, 1), (1, 0)]
    full_weight = gather_weight(weight)
    send = prep(key, value, spectra.reshape((4,) + spectra.shape[2:]))
    send = send.reshape(NSEQ, -1, send.shape[1])
    received = lax.all_to_all(send, SEQ, split_axis=0, concat_axis=0, tiled=True)
    y = convolve(received.reshape(-1, received.shape[2]))
    y = lax.all_to_all(y.reshape(NSEQ, -1, TOK), SEQ, split_axis=0, concat_axis=0, tiled=True)
    gated = gate(y.reshape(-1, TOK), query, key, value, gain[None, :])
    over_h = lax.ppermute(gated, "h", swap)
    over_k = lax.ppermute(gated, "k", swap)
    over_hk = lax.ppermute(over_h, "k", swap)
    h, k = lax.axis_index("h"), lax.axis_index("k")
    order = jnp.stack([h * 2 + k, h * 2 + 1 - k, (1 - h) * 2 + k, (1 - h) * 2 + 1 - k])
    return project(order.astype(jnp.int32), (gated, over_k, over_h, over_hk), full_weight)


def solution(mesh):
    fine = Mesh(mesh.devices.reshape(4, 4, 4, 2, 2), ("y", "z", "x", "h", "k"))
    chan = ("h", "k")
    return jax.shard_map(
        local,
        mesh=fine,
        in_specs=(
            P(SEQ, chan),
            P(SEQ, chan),
            P(SEQ, chan),
            P(None, SEQ, None, chan),
            P(chan),
            P(chan + SEQ, None),
        ),
        out_specs=P(SEQ, chan),
        check_vma=False,
    )
```

```python
import functools

import numpy as np

import jax
import jax.numpy as jnp
import ml_dtypes
from jax import lax
from jax.experimental import pallas as pl
from jax.experimental.pallas import tpu as pltpu
from jax.sharding import Mesh, PartitionSpec as P

BF, F32 = jnp.bfloat16, jnp.float32
SEQ = ("y", "z", "x")
TOK, NSEQ, CLASSES = 256, 64, 128
FULL = CLASSES * TOK
BIG = 56 << 20
SMALL = 16 << 20
KEPT = 72


def split(table):
    hi = table.astype(ml_dtypes.bfloat16)
    lo = (table - hi.astype(np.float64)).astype(ml_dtypes.bfloat16)
    return hi, lo


def tables():
    classes = np.concatenate([np.arange(0, CLASSES, 2), np.arange(1, CLASSES, 2)])
    blocks, rows = np.arange(NSEQ), np.arange(TOK)
    kept = np.arange(KEPT)
    real = (kept <= CLASSES // 2)[:, None]
    same = (kept[:, None] == classes[None, :]) & real
    other = (CLASSES - kept[:, None] == classes[None, :]) & real & ~same
    fold = np.stack([1.0 * same + other, 1.0 * same - other]).astype(ml_dtypes.bfloat16)
    turn = 2 * np.pi * (kept[:, None] * blocks[None, :] % CLASSES) / CLASSES
    cos, sin = np.cos(turn) * real, np.sin(turn) * real
    fwd_hi, fwd_lo = split(np.concatenate([cos, -sin], 0))
    first = np.concatenate([fwd_hi, fwd_lo], 1)
    last = np.concatenate(split(np.concatenate([cos.T, -sin.T], 1) / FULL), 0)
    turn = 2 * np.pi * (rows[:, None] * rows[None, :] % TOK) / TOK
    row_hi, row_lo = split(np.concatenate([np.cos(turn), np.sin(turn)], 0))
    row = np.concatenate([row_hi, row_hi, row_lo], 0)
    turn = 2 * np.pi * (kept[:, None] * rows[None, :]) / FULL
    return fold, first, last, row, np.stack([np.cos(turn), np.sin(turn)]).astype(np.float32)


def dot(a, b):
    return lax.dot_general(a, b, (((1,), (0,)), ((), ())), preferred_element_type=F32)


def parts(value):
    hi = value.astype(BF)
    return hi, (value - hi.astype(F32)).astype(BF)


def prep_kernel(turned_ref, k_ref, v_ref, s_ref, o_ref):
    conv = k_ref[...].astype(F32) * v_ref[...].astype(F32)
    o_ref[:, :TOK] = conv.T.astype(BF)
    row = lax.broadcasted_iota(jnp.int32, (TOK, TOK), 0)
    col = lax.broadcasted_iota(jnp.int32, (TOK, TOK), 1)
    for e in range(2):
        place = jnp.where(turned_ref[e] == 1, TOK - 1 - row, row)
        order = jnp.where(place == col, 1.0, 0.0).astype(BF)
        for j in (e, 2 + e):
            o_ref[:, TOK * (j + 1) : TOK * (j + 2)] = dot(s_ref[j].T.astype(BF), order).astype(BF)


def prep(turned, key, value, spectra):
    width = key.shape[1]
    blk = 512
    tok = pl.BlockSpec((TOK, blk), lambda i, turned: (0, i))
    return pl.pallas_call(
        prep_kernel,
        grid_spec=pltpu.PrefetchScalarGridSpec(
            num_scalar_prefetch=1,
            grid=(width // blk,),
            in_specs=[tok, tok, pl.BlockSpec((4, TOK, blk), lambda i, turned: (0, 0, i))],
            out_specs=pl.BlockSpec((blk, 5 * TOK), lambda i, turned: (i, 0)),
        ),
        out_shape=jax.ShapeDtypeStruct((width, 5 * TOK), BF),
        compiler_params=pltpu.CompilerParams(vmem_limit_bytes=BIG),
        name="prep",
    )(turned, key, value, spectra)


GROUP = 8


def widen(src, dst, columns):
    def chunk(i, _):
        rows = pl.ds(pl.multiple_of(i * 64, 64), 64)
        for c in range(columns):
            dst[c, rows, :] = src[rows, c * 128 : c * 128 + 128].astype(F32)
        return 0

    lax.fori_loop(0, src.shape[0] // 64, chunk, 0)


def rows_of(ref, h, chans, col):
    rows = pl.ds(h, NSEQ, stride=chans)
    return jnp.concatenate([ref[2 * col, rows, :], ref[2 * col + 1, rows, :]], 1)


def row_section(stacked, row_ref):
    hi = jnp.concatenate([piece for pieces in stacked[0::2] for piece in pieces], 0)
    lo = jnp.concatenate([piece for pieces in stacked[1::2] for piece in pieces], 0)
    return dot(jnp.concatenate([hi, lo, hi], 1), row_ref[...])


def fetch(pairs, sems):
    copies = [pltpu.make_async_copy(src, dst, sems.at[i]) for i, (src, dst) in enumerate(pairs)]
    for copy in copies:
        copy.start()
    return copies


def convolve_kernel(group, r_ref, fold_any, first_any, last_any, row_any, turn_any, o_ref, xs, ys, fold_ref, first_ref, last_ref, row_ref, turn_ref, sems):
    chans = r_ref.shape[0] // NSEQ
    copies = fetch(
        [(fold_any, fold_ref), (first_any, first_ref), (last_any, last_ref), (row_any, row_ref), (turn_any, turn_ref)],
        sems,
    )
    widen(r_ref, xs, 10)
    for copy in copies:
        copy.wait()

    def response(h, part):
        pair = [rows_of(xs, h, chans, 1 + 2 * part + e).astype(BF) for e in range(2)]
        return dot(fold_ref[part], jnp.concatenate(pair, 0))

    def step(g, _):
        tc, ts = turn_ref[0], turn_ref[1]
        stacked = []
        for j in range(group):
            x = rows_of(xs, g * group + j, chans, 0).astype(BF)
            a = dot(first_ref[...], jnp.concatenate([x, x], 0))
            ar, ai = a[:KEPT], a[KEPT:]
            ar, ai = parts(ar * tc + ai * ts), parts(ai * tc - ar * ts)
            stacked += [[jnp.concatenate([ar[n], ai[n]], 1), jnp.concatenate([ai[n], -ar[n]], 1)] for n in (0, 1)]
        freq = row_section(stacked, row_ref)
        stacked = []
        for j in range(group):
            h = g * group + j
            rr, ri = response(h, 0), response(h, 1)
            base = 2 * KEPT * j
            xr, xi = freq[base : base + KEPT], freq[base + KEPT : base + 2 * KEPT]
            pr, pi = parts(rr * xr - ri * xi), parts(rr * xi + ri * xr)
            stacked += [[jnp.concatenate([pr[n], -pi[n]], 1), jnp.concatenate([pi[n], pr[n]], 1)] for n in (0, 1)]
        back = row_section(stacked, row_ref)
        for j in range(group):
            h = g * group + j
            base = 2 * KEPT * j
            br, bi = back[base : base + KEPT], back[base + KEPT : base + 2 * KEPT]
            hi, lo = parts(jnp.concatenate([br * tc - bi * ts, bi * tc + br * ts], 0))
            both = dot(last_ref[...], hi)
            y = both[:NSEQ] + both[NSEQ:] + dot(last_ref[:NSEQ], lo)
            for c in range(2):
                ys[c, pl.ds(h, NSEQ, stride=chans), :] = y[:, c * 128 : c * 128 + 128]
        return 0

    lax.fori_loop(0, chans // group, step, 0)
    for c in range(2):
        o_ref[:, c * 128 : c * 128 + 128] = ys[c].astype(BF)


VMEM = pl.BlockSpec(memory_space=pltpu.VMEM)
ANY = pl.BlockSpec(memory_space=pl.ANY)


def constants():
    return [jnp.asarray(table) for table in tables()]


def held(consts):
    return [pltpu.VMEM(c.shape, c.dtype) for c in consts]


def block(shape):
    return pl.BlockSpec(shape, lambda i: (0,) * len(shape))


def convolve(received, group=GROUP):
    rows = received.shape[0]
    consts = constants()
    return pl.pallas_call(
        functools.partial(convolve_kernel, group),
        grid=(1,),
        in_specs=[block(received.shape)] + [ANY] * len(consts),
        out_specs=block((rows, TOK)),
        out_shape=jax.ShapeDtypeStruct((rows, TOK), BF),
        scratch_shapes=[pltpu.VMEM((10, rows, 128), F32), pltpu.VMEM((2, rows, 128), F32)]
        + held(consts)
        + [pltpu.SemaphoreType.DMA((len(consts),))],
        compiler_params=pltpu.CompilerParams(vmem_limit_bytes=BIG),
        name="convolve",
    )(received, *consts)


def prep_g_kernel(q_ref, k_ref, v_ref, s_ref, qt_ref, ct_ref):
    conv = k_ref[...].astype(F32) * v_ref[...].astype(F32)
    qt_ref[...] = q_ref[...].astype(F32).T.astype(BF)
    ct_ref[...] = (s_ref[...] * conv).T


def prep_g(query, key, value, gain):
    width = key.shape[1]
    blk = 512
    tok = pl.BlockSpec((TOK, blk), lambda i: (0, i))
    chan = pl.BlockSpec((blk, TOK), lambda i: (i, 0))
    return pl.pallas_call(
        prep_g_kernel,
        grid=(width // blk,),
        in_specs=[tok, tok, tok, pl.BlockSpec((1, blk), lambda i: (0, i))],
        out_specs=[chan, chan],
        out_shape=[jax.ShapeDtypeStruct((width, TOK), BF), jax.ShapeDtypeStruct((width, TOK), F32)],
        compiler_params=pltpu.CompilerParams(vmem_limit_bytes=SMALL),
        cost_estimate=pl.CostEstimate(flops=1 << 20, bytes_accessed=4 << 20, transcendentals=0),
        name="prep_g",
    )(query, key, value, gain)


def gate_kernel(y_ref, q_ref, c_ref, o_ref):
    o_ref[...] = (q_ref[...].astype(F32) * (y_ref[...].astype(F32) + c_ref[...])).astype(BF)


def gate(y, query_t, direct_t):
    width = y.shape[0]
    blk = 512
    chan = pl.BlockSpec((blk, TOK), lambda i: (i, 0))
    return pl.pallas_call(
        gate_kernel,
        grid=(width // blk,),
        in_specs=[chan] * 3,
        out_specs=chan,
        out_shape=jax.ShapeDtypeStruct((width, TOK), BF),
        compiler_params=pltpu.CompilerParams(vmem_limit_bytes=SMALL),
        name="gate",
    )(y, query_t, direct_t)


def project_kernel(count, more, final, order_ref, *refs):
    g_refs, w_refs, o_ref = refs[:count], refs[count : 2 * count], refs[-1]
    for y in range(w_refs[0].shape[0]):
        lines = slice(y * 256, y * 256 + 256)
        total = refs[-2][lines] if more else None
        for g_ref, w_ref in zip(g_refs, w_refs):
            w = jnp.concatenate([w_ref[y, x, (order_ref[count] - z) & 3] for z in range(4) for x in range(4)], 0)
            term = dot(w, g_ref[...])
            total = term if total is None else total + term
        if final:
            o_ref[:, lines] = total.T.astype(BF)
        else:
            o_ref[lines] = total


def project(order, pieces, weight, base=None):
    final = base is not None
    width = pieces[0].shape[0]
    count, steps = len(pieces), 2
    lines = 1024 // steps
    more = [base] if final else []
    whole = pl.BlockSpec((width, TOK), lambda i, order: (0, 0))
    sums = pl.BlockSpec((lines, TOK), lambda i, order: (i, 0))
    shape = jax.ShapeDtypeStruct((TOK, 1024) if final else (1024, TOK), BF if final else F32)

    def columns(j):
        shape = (4 // steps,) + weight.shape[1:4] + (width,)
        return pl.BlockSpec(shape, lambda i, order: (i, 0, 0, 0, order[j]))

    return pl.pallas_call(
        functools.partial(project_kernel, count, final, final),
        grid_spec=pltpu.PrefetchScalarGridSpec(
            num_scalar_prefetch=1,
            grid=(steps,),
            in_specs=[whole] * count + [columns(j) for j in range(count)] + [sums] * len(more),
            out_specs=pl.BlockSpec((TOK, lines), lambda i, order: (0, i)) if final else sums,
        ),
        out_shape=shape,
        compiler_params=pltpu.CompilerParams(vmem_limit_bytes=SMALL),
        cost_estimate=pl.CostEstimate(flops=1 << 35, bytes_accessed=6 << 20, transcendentals=0),
        name="project_last" if final else "project_first",
    )(order, *pieces, *([weight] * count), *more)


def gather_weight(weight, after):
    pieces = [weight] + [
        lax.ppermute(weight, "z", [(a, (a + d) % 4) for a in range(4)]) for d in (1, 2, 3)
    ]
    *pieces, after = lax.optimization_barrier((*pieces, after))
    full = lax.all_gather(jnp.stack(pieces)[None], ("y", "x"), axis=0, tiled=True)
    return full.reshape((4, 4, 4) + weight.shape), after


def exchange(send):
    send = send.reshape(NSEQ, -1, send.shape[1])
    got = lax.all_to_all(send, SEQ, split_axis=0, concat_axis=0, tiled=True)
    return got.reshape(-1, got.shape[2])


def local(query, key, value, spectra, gain, weight):
    swap = [(0, 1), (1, 0)]
    index = (lax.axis_index("y") * 4 + lax.axis_index("z")) * 4 + lax.axis_index("x")
    turned = (2 * index + jnp.arange(2) > CLASSES // 2).astype(jnp.int32)
    send = prep(turned, key, value, spectra.reshape((4,) + spectra.shape[2:]))
    full_weight, send = gather_weight(weight, send)
    send, query, key, value, gain = lax.optimization_barrier((send, query, key, value, gain))
    got = exchange(send)
    query_t, direct_t = prep_g(query, key, value, gain[None, :])
    y = exchange(convolve(got))
    gated = gate(y, query_t, direct_t)
    over_k = lax.ppermute(gated, "k", swap)
    gated, over_k = lax.optimization_barrier((gated, over_k))
    over_h = lax.ppermute(gated, "h", swap)
    h, k, z = lax.axis_index("h"), lax.axis_index("k"), lax.axis_index("z")
    near = jnp.stack([h * 2 + k, h * 2 + 1 - k, z]).astype(jnp.int32)
    far = jnp.stack([(1 - h) * 2 + k, (1 - h) * 2 + 1 - k, z]).astype(jnp.int32)
    near, far = lax.optimization_barrier((near, far))
    total = project(near, (gated, over_k), full_weight)
    over_h, total = lax.optimization_barrier((over_h, total))
    over_hk = lax.ppermute(over_h, "k", swap)
    return project(far, (over_h, over_hk), full_weight, total)


def solution(mesh):
    fine = Mesh(mesh.devices.reshape(4, 4, 4, 2, 2), ("y", "z", "x", "h", "k"))
    chan = ("h", "k")
    return jax.shard_map(
        local,
        mesh=fine,
        in_specs=(
            P(SEQ, chan),
            P(SEQ, chan),
            P(SEQ, chan),
            P(None, SEQ, None, chan),
            P(chan),
            P(chan + SEQ, None),
        ),
        out_specs=P(SEQ, chan),
        check_vma=False,
    )
```

```python
import functools

import numpy as np

import jax
import jax.numpy as jnp
import ml_dtypes
from jax import lax
from jax.experimental import pallas as pl
from jax.experimental.pallas import tpu as pltpu
from jax.sharding import Mesh, PartitionSpec as P

BF, F32 = jnp.bfloat16, jnp.float32
SEQ = ("y", "z", "x")
TOK, NSEQ, CLASSES = 256, 64, 128
FULL = CLASSES * TOK
BIG = 56 << 20
SMALL = 16 << 20
KEPT = 72


def split(table):
    hi = table.astype(ml_dtypes.bfloat16)
    lo = (table - hi.astype(np.float64)).astype(ml_dtypes.bfloat16)
    return hi, lo


def tables():
    classes = np.concatenate([np.arange(0, CLASSES, 2), np.arange(1, CLASSES, 2)])
    blocks, rows = np.arange(NSEQ), np.arange(TOK)
    kept = np.arange(KEPT)
    real = (kept <= CLASSES // 2)[:, None]
    same = (kept[:, None] == classes[None, :]) & real
    other = (CLASSES - kept[:, None] == classes[None, :]) & real & ~same
    fold = np.stack([1.0 * same + other, 1.0 * same - other]).astype(ml_dtypes.bfloat16)
    turn = 2 * np.pi * (kept[:, None] * blocks[None, :] % CLASSES) / CLASSES
    cos, sin = np.cos(turn) * real, np.sin(turn) * real
    fwd_hi, fwd_lo = split(np.concatenate([cos, -sin], 0))
    first = np.concatenate([fwd_hi, fwd_lo], 1)
    last = np.concatenate(split(np.concatenate([cos.T, -sin.T], 1) / FULL), 0)
    turn = 2 * np.pi * (rows[:, None] * rows[None, :] % TOK) / TOK
    row_hi, row_lo = split(np.concatenate([np.cos(turn), np.sin(turn)], 0))
    row = np.concatenate([row_hi, row_hi, row_lo], 0)
    turn = 2 * np.pi * (kept[:, None] * rows[None, :]) / FULL
    return fold, first, last, row, np.stack([np.cos(turn), np.sin(turn)]).astype(np.float32)


def dot(a, b):
    return lax.dot_general(a, b, (((1,), (0,)), ((), ())), preferred_element_type=F32)


def parts(value):
    hi = value.astype(BF)
    return hi, (value - hi.astype(F32)).astype(BF)


def prep_kernel(turned_ref, k_ref, v_ref, s_ref, o_ref):
    conv = k_ref[...].astype(F32) * v_ref[...].astype(F32)
    o_ref[:, :TOK] = conv.T.astype(BF)
    row = lax.broadcasted_iota(jnp.int32, (TOK, TOK), 0)
    col = lax.broadcasted_iota(jnp.int32, (TOK, TOK), 1)
    for e in range(2):
        place = jnp.where(turned_ref[e] == 1, TOK - 1 - row, row)
        order = jnp.where(place == col, 1.0, 0.0).astype(BF)
        for j in (e, 2 + e):
            o_ref[:, TOK * (j + 1) : TOK * (j + 2)] = dot(s_ref[j].T.astype(BF), order).astype(BF)


def prep(turned, key, value, spectra):
    width = key.shape[1]
    blk = 512
    tok = pl.BlockSpec((TOK, blk), lambda i, turned: (0, i))
    return pl.pallas_call(
        prep_kernel,
        grid_spec=pltpu.PrefetchScalarGridSpec(
            num_scalar_prefetch=1,
            grid=(width // blk,),
            in_specs=[tok, tok, pl.BlockSpec((4, TOK, blk), lambda i, turned: (0, 0, i))],
            out_specs=pl.BlockSpec((blk, 5 * TOK), lambda i, turned: (i, 0)),
        ),
        out_shape=jax.ShapeDtypeStruct((width, 5 * TOK), BF),
        compiler_params=pltpu.CompilerParams(vmem_limit_bytes=BIG),
        name="prep",
    )(turned, key, value, spectra)


GROUP = 8


def widen(src, dst, columns):
    def chunk(i, _):
        rows = pl.ds(pl.multiple_of(i * 64, 64), 64)
        for c in range(columns):
            dst[c, rows, :] = src[rows, c * 128 : c * 128 + 128].astype(F32)
        return 0

    lax.fori_loop(0, src.shape[0] // 64, chunk, 0)


def rows_of(ref, h, chans, col):
    rows = pl.ds(h, NSEQ, stride=chans)
    return jnp.concatenate([ref[2 * col, rows, :], ref[2 * col + 1, rows, :]], 1)


def row_section(stacked, row_ref):
    hi = jnp.concatenate([piece for pieces in stacked[0::2] for piece in pieces], 0)
    lo = jnp.concatenate([piece for pieces in stacked[1::2] for piece in pieces], 0)
    return dot(jnp.concatenate([hi, lo, hi], 1), row_ref[...])


def fetch(pairs, sems):
    copies = [pltpu.make_async_copy(src, dst, sems.at[i]) for i, (src, dst) in enumerate(pairs)]
    for copy in copies:
        copy.start()
    return copies


def convolve_kernel(group, r_ref, fold_any, first_any, last_any, row_any, turn_any, o_ref, xs, ys, fold_ref, first_ref, last_ref, row_ref, turn_ref, sems):
    chans = r_ref.shape[0] // NSEQ
    copies = fetch(
        [(fold_any, fold_ref), (first_any, first_ref), (last_any, last_ref), (row_any, row_ref), (turn_any, turn_ref)],
        sems,
    )
    widen(r_ref, xs, 10)
    for copy in copies:
        copy.wait()

    def response(h, part):
        pair = [rows_of(xs, h, chans, 1 + 2 * part + e).astype(BF) for e in range(2)]
        return dot(fold_ref[part], jnp.concatenate(pair, 0))

    def step(g, _):
        tc, ts = turn_ref[0], turn_ref[1]
        stacked = []
        for j in range(group):
            x = rows_of(xs, g * group + j, chans, 0).astype(BF)
            a = dot(first_ref[...], jnp.concatenate([x, x], 0))
            ar, ai = a[:KEPT], a[KEPT:]
            ar, ai = parts(ar * tc + ai * ts), parts(ai * tc - ar * ts)
            stacked += [[jnp.concatenate([ar[n], ai[n]], 1), jnp.concatenate([ai[n], -ar[n]], 1)] for n in (0, 1)]
        freq = row_section(stacked, row_ref)
        stacked = []
        for j in range(group):
            h = g * group + j
            rr, ri = response(h, 0), response(h, 1)
            base = 2 * KEPT * j
            xr, xi = freq[base : base + KEPT], freq[base + KEPT : base + 2 * KEPT]
            pr, pi = parts(rr * xr - ri * xi), parts(rr * xi + ri * xr)
            stacked += [[jnp.concatenate([pr[n], -pi[n]], 1), jnp.concatenate([pi[n], pr[n]], 1)] for n in (0, 1)]
        back = row_section(stacked, row_ref)
        for j in range(group):
            h = g * group + j
            base = 2 * KEPT * j
            br, bi = back[base : base + KEPT], back[base + KEPT : base + 2 * KEPT]
            hi, lo = parts(jnp.concatenate([br * tc - bi * ts, bi * tc + br * ts], 0))
            both = dot(last_ref[...], hi)
            y = both[:NSEQ] + both[NSEQ:] + dot(last_ref[:NSEQ], lo)
            for c in range(2):
                ys[c, pl.ds(h, NSEQ, stride=chans), :] = y[:, c * 128 : c * 128 + 128]
        return 0

    lax.fori_loop(0, chans // group, step, 0)
    for c in range(2):
        o_ref[:, c * 128 : c * 128 + 128] = ys[c].astype(BF)


VMEM = pl.BlockSpec(memory_space=pltpu.VMEM)
ANY = pl.BlockSpec(memory_space=pl.ANY)


def constants():
    return [jnp.asarray(table) for table in tables()]


def held(consts):
    return [pltpu.VMEM(c.shape, c.dtype) for c in consts]


def block(shape):
    return pl.BlockSpec(shape, lambda i: (0,) * len(shape))


def convolve(received, group=GROUP):
    rows = received.shape[0]
    consts = constants()
    return pl.pallas_call(
        functools.partial(convolve_kernel, group),
        grid=(1,),
        in_specs=[block(received.shape)] + [ANY] * len(consts),
        out_specs=block((rows, TOK)),
        out_shape=jax.ShapeDtypeStruct((rows, TOK), BF),
        scratch_shapes=[pltpu.VMEM((10, rows, 128), F32), pltpu.VMEM((2, rows, 128), F32)]
        + held(consts)
        + [pltpu.SemaphoreType.DMA((len(consts),))],
        compiler_params=pltpu.CompilerParams(vmem_limit_bytes=BIG),
        cost_estimate=pl.CostEstimate(flops=16 << 30, bytes_accessed=4 << 20, transcendentals=0),
        name="convolve",
    )(received, *consts)


def prep_g_kernel(q_ref, k_ref, v_ref, s_ref, qt_ref, ct_ref):
    conv = k_ref[...].astype(F32) * v_ref[...].astype(F32)
    qt_ref[...] = q_ref[...].astype(F32).T.astype(BF)
    ct_ref[...] = (s_ref[...] * conv).T


def prep_g(query, key, value, gain):
    width = key.shape[1]
    blk = 512
    tok = pl.BlockSpec((TOK, blk), lambda i: (0, i))
    chan = pl.BlockSpec((blk, TOK), lambda i: (i, 0))
    return pl.pallas_call(
        prep_g_kernel,
        grid=(width // blk,),
        in_specs=[tok, tok, tok, pl.BlockSpec((1, blk), lambda i: (0, i))],
        out_specs=[chan, chan],
        out_shape=[jax.ShapeDtypeStruct((width, TOK), BF), jax.ShapeDtypeStruct((width, TOK), F32)],
        compiler_params=pltpu.CompilerParams(vmem_limit_bytes=SMALL),
        cost_estimate=pl.CostEstimate(flops=1 << 20, bytes_accessed=4 << 20, transcendentals=0),
        name="prep_g",
    )(query, key, value, gain)


def gate_kernel(y_ref, q_ref, c_ref, o_ref):
    o_ref[...] = (q_ref[...].astype(F32) * (y_ref[...].astype(F32) + c_ref[...])).astype(BF)


def gate(y, query_t, direct_t):
    width = y.shape[0]
    blk = 512
    chan = pl.BlockSpec((blk, TOK), lambda i: (i, 0))
    return pl.pallas_call(
        gate_kernel,
        grid=(width // blk,),
        in_specs=[chan] * 3,
        out_specs=chan,
        out_shape=jax.ShapeDtypeStruct((width, TOK), BF),
        compiler_params=pltpu.CompilerParams(vmem_limit_bytes=SMALL),
        name="gate",
    )(y, query_t, direct_t)


def sum_terms(g_refs, w_refs, total):
    own, left, opp0, opp1, right = w_refs
    for d, pair in enumerate(((own, own), (left, left), (opp0, opp1), (right, right))):
        terms = []
        for c, (g_ref, w_ref) in enumerate(zip(g_refs, pair)):
            w = w_ref[...] if d == 2 else w_ref[c]
            terms.append(dot(w.reshape(256, w.shape[-1]), g_ref[...]))
        total[d * 256 : d * 256 + 256, :] = terms[0] + terms[1]


def near_kernel(g0, g1, own, left, opp0, opp1, right, o_ref):
    sum_terms((g0, g1), (own, left, opp0, opp1, right), o_ref)


def far_kernel(place_ref, g0, g1, own, left, opp0, opp1, right, near_ref, o_ref, total):
    sum_terms((g0, g1), (own, left, opp0, opp1, right), total)

    def line(ref, a, b, c):
        return ref[pl.ds(pl.multiple_of(((a * 4 + b) * 4 + c) * 16, 16), 16), :]

    for y in range(4):
        dy, pieces = (place_ref[0] - y) & 3, []
        for z in range(4):
            for x in range(4):
                dz, dx = (place_ref[1] - z) & 3, (place_ref[2] - x) & 3
                pieces.append(line(near_ref, dx, dy, dz) + line(total, dy, dx, dz))
        o_ref[:, y * 256 : y * 256 + 256] = jnp.concatenate(pieces, 0).T.astype(BF)


def project(place, pieces, weights, near=None):
    own, left, (opp0, opp1), right = weights
    args = [*pieces, own, left, opp0, opp1, right] + ([] if near is None else [near])

    def whole(shape):
        return pl.BlockSpec(shape, lambda i, *_: (0,) * len(shape))

    shape, kind = ((1024, TOK), F32) if near is None else ((TOK, 1024), BF)
    return pl.pallas_call(
        near_kernel if near is None else far_kernel,
        grid_spec=pltpu.PrefetchScalarGridSpec(
            num_scalar_prefetch=0 if near is None else 1,
            grid=(1,),
            in_specs=[whole(a.shape) for a in args],
            out_specs=whole(shape),
            scratch_shapes=[] if near is None else [pltpu.VMEM((1024, TOK), F32)],
        ),
        out_shape=jax.ShapeDtypeStruct(shape, kind),
        compiler_params=pltpu.CompilerParams(vmem_limit_bytes=24 << 20),
        cost_estimate=pl.CostEstimate(flops=1 << 35, bytes_accessed=6 << 20, transcendentals=0),
        name="near" if near is None else "far",
    )(*([] if near is None else [place]), *args)


def ring(axis, step):
    return axis, [(a, (a + step) % 4) for a in range(4)]


def beside(piece, axis):
    return lax.ppermute(piece, *ring(axis, 1)), lax.ppermute(piece, *ring(axis, -1))


def opposite(left, right, axis):
    return lax.ppermute(left, *ring(axis, 1)), lax.ppermute(right, *ring(axis, -1))


def around(piece, axis):
    left, right = beside(piece, axis)
    return piece, left, opposite(left[0], right[1], axis), right


def stacked(pieces):
    own, left, (opp0, opp1), right = pieces
    return jnp.stack([jnp.stack([own[c], left[c], opp, right[c]]) for c, opp in enumerate((opp0, opp1))])


def gather_weight(weight, chan, after):
    pieces = [weight] + [
        lax.ppermute(weight, "z", [(a, (a + d) % 4) for a in range(4)]) for d in (1, 2, 3)
    ]
    *pieces, after = lax.optimization_barrier((*pieces, after))
    width = weight.shape[1] // 4
    rows = jnp.stack(pieces)
    near, far = [
        jnp.stack([lax.dynamic_slice_in_dim(rows, (chan ^ j) * width, width, 2) for j in pair])
        for pair in ((0, 1), (2, 3))
    ]
    far = stacked(around(far, "x"))
    near = stacked(around(near, "y"))
    return (near, *beside(near, "x")), (far, *beside(far, "y")), after


def exchange(send):
    send = send.reshape(NSEQ, -1, send.shape[1])
    got = lax.all_to_all(send, SEQ, split_axis=0, concat_axis=0, tiled=True)
    return got.reshape(-1, got.shape[2])


def local(query, key, value, spectra, gain, weight):
    swap = [(0, 1), (1, 0)]
    index = (lax.axis_index("y") * 4 + lax.axis_index("z")) * 4 + lax.axis_index("x")
    turned = (2 * index + jnp.arange(2) > CLASSES // 2).astype(jnp.int32)
    send = prep(turned, key, value, spectra.reshape((4,) + spectra.shape[2:]))
    h, k = lax.axis_index("h"), lax.axis_index("k")
    (near_own, *near), (far_own, *far), send = gather_weight(weight, h * 2 + k, send)
    send, query, key, value, gain = lax.optimization_barrier((send, query, key, value, gain))
    got = exchange(send)
    query_t, direct_t = prep_g(query, key, value, gain[None, :])
    y = convolve(got)
    y, near, far = lax.optimization_barrier((y, near, far))
    y = exchange(y)
    opposites = opposite(near[0][0], near[1][1], "x")
    relay = far[0][0], far[1][1]
    y, opposites, relay = lax.optimization_barrier((y, opposites, relay))
    near_weight = near_own, near[0], opposites, near[1]
    gated = gate(y, query_t, direct_t)
    over_k = lax.ppermute(gated, "k", swap)
    over_h = lax.ppermute(gated, "h", swap)
    over_k, relay = lax.optimization_barrier((over_k, relay))
    place = jnp.stack([lax.axis_index(axis) for axis in ("y", "z", "x")]).astype(jnp.int32)
    total = project(place, (gated, over_k), near_weight)
    over_h, total = lax.optimization_barrier((over_h, total))
    over_hk = lax.ppermute(over_h, "k", swap)
    far_weight = far_own, far[0], opposite(*relay, "y"), far[1]
    return project(place, (over_h, over_hk), far_weight, total)


def solution(mesh):
    fine = Mesh(mesh.devices.reshape(4, 4, 4, 2, 2), ("y", "z", "x", "h", "k"))
    chan = ("h", "k")
    return jax.shard_map(
        local,
        mesh=fine,
        in_specs=(
            P(SEQ, chan),
            P(SEQ, chan),
            P(SEQ, chan),
            P(None, SEQ, None, chan),
            P(chan),
            P(chan + SEQ, None),
        ),
        out_specs=P(SEQ, chan),
        check_vma=False,
    )
```

```python
import functools

import numpy as np

import jax
import jax.numpy as jnp
import ml_dtypes
from jax import lax
from jax.experimental import pallas as pl
from jax.experimental.pallas import tpu as pltpu
from jax.sharding import Mesh, PartitionSpec as P

BF, F32 = jnp.bfloat16, jnp.float32
SEQ = ("y", "z", "x")
TOK, NSEQ, CLASSES = 256, 64, 128
FULL = CLASSES * TOK
BIG = 56 << 20
SMALL = 16 << 20
KEPT = 72
GATE = 256


def split(table):
    hi = table.astype(ml_dtypes.bfloat16)
    lo = (table - hi.astype(np.float64)).astype(ml_dtypes.bfloat16)
    return hi, lo


def tables():
    classes = np.concatenate([np.arange(0, CLASSES, 2), np.arange(1, CLASSES, 2)])
    blocks, rows = np.arange(NSEQ), np.arange(TOK)
    kept = np.arange(KEPT)
    real = (kept <= CLASSES // 2)[:, None]
    same = (kept[:, None] == classes[None, :]) & real
    other = (CLASSES - kept[:, None] == classes[None, :]) & real & ~same
    fold = np.stack([1.0 * same + other, 1.0 * same - other]).astype(ml_dtypes.bfloat16)
    turn = 2 * np.pi * (kept[:, None] * blocks[None, :] % CLASSES) / CLASSES
    cos, sin = np.cos(turn) * real, np.sin(turn) * real
    fwd_hi, fwd_lo = split(np.concatenate([cos, -sin], 0))
    first = np.concatenate([fwd_hi, fwd_lo], 1)
    last = np.concatenate(split(np.concatenate([cos.T, -sin.T], 1) / FULL), 0)
    turn = 2 * np.pi * (rows[:, None] * rows[None, :] % TOK) / TOK
    row_hi, row_lo = split(np.concatenate([np.cos(turn), np.sin(turn)], 0))
    row = np.concatenate([row_hi, row_hi, row_lo], 0)
    turn = 2 * np.pi * (kept[:, None] * rows[None, :]) / FULL
    return fold, first, last, row, np.stack([np.cos(turn), np.sin(turn)]).astype(np.float32)


def dot(a, b):
    return lax.dot_general(a, b, (((1,), (0,)), ((), ())), preferred_element_type=F32)


def parts(value):
    hi = value.astype(BF)
    return hi, (value - hi.astype(F32)).astype(BF)


def prep_kernel(turned_ref, k_ref, v_ref, s_ref, o_ref):
    conv = k_ref[...].astype(F32) * v_ref[...].astype(F32)
    o_ref[:, :TOK] = conv.T.astype(BF)
    row = lax.broadcasted_iota(jnp.int32, (TOK, TOK), 0)
    col = lax.broadcasted_iota(jnp.int32, (TOK, TOK), 1)
    for e in range(2):
        place = jnp.where(turned_ref[e] == 1, TOK - 1 - row, row)
        order = jnp.where(place == col, 1.0, 0.0).astype(BF)
        for j in (e, 2 + e):
            o_ref[:, TOK * (j + 1) : TOK * (j + 2)] = dot(s_ref[j].T.astype(BF), order).astype(BF)


def prep(turned, key, value, spectra):
    width = key.shape[1]
    blk = 512
    tok = pl.BlockSpec((TOK, blk), lambda i, turned: (0, i))
    return pl.pallas_call(
        prep_kernel,
        grid_spec=pltpu.PrefetchScalarGridSpec(
            num_scalar_prefetch=1,
            grid=(width // blk,),
            in_specs=[tok, tok, pl.BlockSpec((4, TOK, blk), lambda i, turned: (0, 0, i))],
            out_specs=pl.BlockSpec((blk, 5 * TOK), lambda i, turned: (i, 0)),
        ),
        out_shape=jax.ShapeDtypeStruct((width, 5 * TOK), BF),
        compiler_params=pltpu.CompilerParams(vmem_limit_bytes=BIG),
        name="prep",
    )(turned, key, value, spectra)


GROUP = 8


def widen(src, dst, columns, base):
    def chunk(i, _):
        rows = pl.ds(pl.multiple_of(i * 64, 64), 64)
        for c in range(columns):
            dst[base + c, rows, :] = src[rows, c * 128 : c * 128 + 128].astype(F32)
        return 0

    lax.fori_loop(0, src.shape[0] // 64, chunk, 0)


def rows_of(ref, h, chans, col):
    rows = pl.ds(h, NSEQ, stride=chans)
    return jnp.concatenate([ref[2 * col, rows, :], ref[2 * col + 1, rows, :]], 1)


def row_section(stacked, row_ref):
    hi = jnp.concatenate([piece for pieces in stacked[0::2] for piece in pieces], 0)
    lo = jnp.concatenate([piece for pieces in stacked[1::2] for piece in pieces], 0)
    return dot(jnp.concatenate([hi, lo, hi], 1), row_ref[...])


def fetch(pairs, sems):
    copies = [pltpu.make_async_copy(src, dst, sems.at[i]) for i, (src, dst) in enumerate(pairs)]
    for copy in copies:
        copy.start()
    return copies


def convolve_kernel(r_any, fold_any, first_any, last_any, row_any, turn_any, o_ref, rx, rs, xs, ys, freq, fold_ref, first_ref, last_ref, row_ref, turn_ref, sems):
    chans = rx.shape[0] // NSEQ
    copies = fetch(
        [
            (r_any.at[:, pl.ds(0, TOK)], rx),
            (first_any, first_ref),
            (turn_any, turn_ref),
            (row_any, row_ref),
            (r_any.at[:, pl.ds(TOK, 4 * TOK)], rs),
            (fold_any, fold_ref),
            (last_any, last_ref),
        ],
        sems,
    )
    copies[0].wait()
    widen(rx, xs, 2, 0)
    for copy in copies[1:4]:
        copy.wait()

    def response(h, part):
        pair = [rows_of(xs, h, chans, 1 + 2 * part + e).astype(BF) for e in range(2)]
        return dot(fold_ref[part], jnp.concatenate(pair, 0))

    def ahead(g, _):
        tc, ts = turn_ref[0], turn_ref[1]
        stacked = []
        for j in range(GROUP):
            x = rows_of(xs, g * GROUP + j, chans, 0).astype(BF)
            a = dot(first_ref[...], jnp.concatenate([x, x], 0))
            ar, ai = a[:KEPT], a[KEPT:]
            ar, ai = parts(ar * tc + ai * ts), parts(ai * tc - ar * ts)
            stacked += [[jnp.concatenate([ar[n], ai[n]], 1), jnp.concatenate([ai[n], -ar[n]], 1)] for n in (0, 1)]
        size = GROUP * 2 * KEPT
        freq[pl.ds(pl.multiple_of(g * size, size), size), :] = row_section(stacked, row_ref)
        return 0

    lax.fori_loop(0, chans // GROUP, ahead, 0)
    for copy in copies[4:]:
        copy.wait()
    widen(rs, xs, 8, 2)

    def back(g, _):
        tc, ts = turn_ref[0], turn_ref[1]
        stacked = []
        for j in range(GROUP):
            h = g * GROUP + j
            rr, ri = response(h, 0), response(h, 1)
            base = pl.multiple_of(h * 2 * KEPT, 8)
            xr, xi = freq[pl.ds(base, KEPT), :], freq[pl.ds(base + KEPT, KEPT), :]
            pr, pi = parts(rr * xr - ri * xi), parts(rr * xi + ri * xr)
            stacked += [[jnp.concatenate([pr[n], -pi[n]], 1), jnp.concatenate([pi[n], pr[n]], 1)] for n in (0, 1)]
        rows = row_section(stacked, row_ref)
        for j in range(GROUP):
            h = g * GROUP + j
            base = 2 * KEPT * j
            br, bi = rows[base : base + KEPT], rows[base + KEPT : base + 2 * KEPT]
            hi, lo = parts(jnp.concatenate([br * tc - bi * ts, bi * tc + br * ts], 0))
            both = dot(last_ref[...], hi)
            y = both[:NSEQ] + both[NSEQ:] + dot(last_ref[:NSEQ], lo)
            for c in range(2):
                ys[c, pl.ds(h, NSEQ, stride=chans), :] = y[:, c * 128 : c * 128 + 128]
        return 0

    lax.fori_loop(0, chans // GROUP, back, 0)
    for c in range(2):
        o_ref[:, c * 128 : c * 128 + 128] = ys[c].astype(BF)


VMEM = pl.BlockSpec(memory_space=pltpu.VMEM)
ANY = pl.BlockSpec(memory_space=pl.ANY)


def constants():
    return [jnp.asarray(table) for table in tables()]


def held(consts):
    return [pltpu.VMEM(c.shape, c.dtype) for c in consts]


def block(shape):
    return pl.BlockSpec(shape, lambda i: (0,) * len(shape))


def convolve(received):
    rows = received.shape[0]
    consts = constants()
    return pl.pallas_call(
        convolve_kernel,
        grid=(1,),
        in_specs=[ANY] * (1 + len(consts)),
        out_specs=block((rows, TOK)),
        out_shape=jax.ShapeDtypeStruct((rows, TOK), BF),
        scratch_shapes=[
            pltpu.VMEM((rows, TOK), BF),
            pltpu.VMEM((rows, 4 * TOK), BF),
            pltpu.VMEM((10, rows, 128), F32),
            pltpu.VMEM((2, rows, 128), F32),
            pltpu.VMEM((rows // NSEQ * 2 * KEPT, TOK), F32),
        ]
        + held(consts)
        + [pltpu.SemaphoreType.DMA((2 + len(consts),))],
        compiler_params=pltpu.CompilerParams(vmem_limit_bytes=BIG),
        cost_estimate=pl.CostEstimate(flops=16 << 30, bytes_accessed=4 << 20, transcendentals=0),
        name="convolve",
    )(received, *consts)


def gate_kernel(y_ref, q_ref, k_ref, v_ref, s_ref, o_ref):
    conv = k_ref[...].astype(F32) * v_ref[...].astype(F32)
    direct = (s_ref[...] * conv).T
    o_ref[...] = (q_ref[...].astype(F32).T * (y_ref[...].astype(F32) + direct)).astype(BF)


def gate(y, query, key, value, gain):
    width = y.shape[0]
    blk = GATE
    tok = pl.BlockSpec((TOK, blk), lambda i: (0, i))
    chan = pl.BlockSpec((blk, TOK), lambda i: (i, 0))
    return pl.pallas_call(
        gate_kernel,
        grid=(width // blk,),
        in_specs=[chan, tok, tok, tok, pl.BlockSpec((1, blk), lambda i: (0, i))],
        out_specs=chan,
        out_shape=jax.ShapeDtypeStruct((width, TOK), BF),
        compiler_params=pltpu.CompilerParams(vmem_limit_bytes=SMALL),
        name="gate",
    )(y, query, key, value, gain)


def sum_terms(g_refs, w_refs, total):
    own, left, opp0, opp1, right = w_refs
    for d, pair in enumerate(((own, own), (left, left), (opp0, opp1), (right, right))):
        terms = []
        for c, (g_ref, w_ref) in enumerate(zip(g_refs, pair)):
            w = w_ref[...] if d == 2 else w_ref[c]
            terms.append(dot(w.reshape(256, w.shape[-1]), g_ref[...]))
        total[d * 256 : d * 256 + 256, :] = terms[0] + terms[1]


def near_kernel(g0, g1, own, left, opp0, opp1, right, o_ref):
    sum_terms((g0, g1), (own, left, opp0, opp1, right), o_ref)


def far_kernel(place_ref, g0, g1, own, left, opp0, opp1, right, near_ref, o_ref, total):
    sum_terms((g0, g1), (own, left, opp0, opp1, right), total)

    def line(ref, a, b, c):
        return ref[pl.ds(pl.multiple_of(((a * 4 + b) * 4 + c) * 16, 16), 16), :]

    for y in range(4):
        dy, pieces = (place_ref[0] - y) & 3, []
        for z in range(4):
            for x in range(4):
                dz, dx = (place_ref[1] - z) & 3, (place_ref[2] - x) & 3
                pieces.append(line(near_ref, dx, dy, dz) + line(total, dy, dx, dz))
        o_ref[:, y * 256 : y * 256 + 256] = jnp.concatenate(pieces, 0).T.astype(BF)


def project(place, pieces, weights, near=None):
    own, left, (opp0, opp1), right = weights
    args = [*pieces, own, left, opp0, opp1, right] + ([] if near is None else [near])

    def whole(shape):
        return pl.BlockSpec(shape, lambda i, *_: (0,) * len(shape))

    shape, kind = ((1024, TOK), F32) if near is None else ((TOK, 1024), BF)
    return pl.pallas_call(
        near_kernel if near is None else far_kernel,
        grid_spec=pltpu.PrefetchScalarGridSpec(
            num_scalar_prefetch=0 if near is None else 1,
            grid=(1,),
            in_specs=[whole(a.shape) for a in args],
            out_specs=whole(shape),
            scratch_shapes=[] if near is None else [pltpu.VMEM((1024, TOK), F32)],
        ),
        out_shape=jax.ShapeDtypeStruct(shape, kind),
        compiler_params=pltpu.CompilerParams(vmem_limit_bytes=24 << 20),
        cost_estimate=pl.CostEstimate(flops=1 << 35, bytes_accessed=6 << 20, transcendentals=0),
        name="near" if near is None else "far",
    )(*([] if near is None else [place]), *args)


def ring(axis, step):
    return axis, [(a, (a + step) % 4) for a in range(4)]


def beside(piece, axis):
    return lax.ppermute(piece, *ring(axis, 1)), lax.ppermute(piece, *ring(axis, -1))


def opposite(left, right, axis):
    return lax.ppermute(left, *ring(axis, 1)), lax.ppermute(right, *ring(axis, -1))


def around(piece, axis):
    left, right = beside(piece, axis)
    return piece, left, opposite(left[0], right[1], axis), right


def stacked(pieces):
    own, left, (opp0, opp1), right = pieces
    return jnp.stack([jnp.stack([own[c], left[c], opp, right[c]]) for c, opp in enumerate((opp0, opp1))])


def gather_weight(weight, chan, after):
    pieces = [weight] + [
        lax.ppermute(weight, "z", [(a, (a + d) % 4) for a in range(4)]) for d in (1, 2, 3)
    ]
    *pieces, after = lax.optimization_barrier((*pieces, after))
    width = weight.shape[1] // 4
    rows = jnp.stack(pieces)
    near, far = [
        jnp.stack([lax.dynamic_slice_in_dim(rows, (chan ^ j) * width, width, 2) for j in pair])
        for pair in ((0, 1), (2, 3))
    ]
    far = stacked(around(far, "x"))
    near = stacked(around(near, "y"))
    return (near, *beside(near, "x")), (far, *beside(far, "y")), after


def exchange(send):
    send = send.reshape(NSEQ, -1, send.shape[1])
    got = lax.all_to_all(send, SEQ, split_axis=0, concat_axis=0, tiled=True)
    return got.reshape(-1, got.shape[2])


def local(query, key, value, spectra, gain, weight):
    swap = [(0, 1), (1, 0)]
    index = (lax.axis_index("y") * 4 + lax.axis_index("z")) * 4 + lax.axis_index("x")
    turned = (2 * index + jnp.arange(2) > CLASSES // 2).astype(jnp.int32)
    send = prep(turned, key, value, spectra.reshape((4,) + spectra.shape[2:]))
    h, k = lax.axis_index("h"), lax.axis_index("k")
    (near_own, *near), (far_own, *far), send = gather_weight(weight, h * 2 + k, send)
    send, query, key, value, gain = lax.optimization_barrier((send, query, key, value, gain))
    got = exchange(send)
    y = convolve(got)
    y, near, far = lax.optimization_barrier((y, near, far))
    y = exchange(y)
    opposites = opposite(near[0][0], near[1][1], "x")
    relay = far[0][0], far[1][1]
    y, relay = lax.optimization_barrier((y, relay))
    gated = gate(y, query, key, value, gain[None, :])
    over_k = lax.ppermute(gated, "k", swap)
    over_h = lax.ppermute(gated, "h", swap)
    over_k, relay, opposites = lax.optimization_barrier((over_k, relay, opposites))
    near_weight = near_own, near[0], opposites, near[1]
    place = jnp.stack([lax.axis_index(axis) for axis in ("y", "z", "x")]).astype(jnp.int32)
    total = project(place, (gated, over_k), near_weight)
    over_h, total = lax.optimization_barrier((over_h, total))
    over_hk = lax.ppermute(over_h, "k", swap)
    far_weight = far_own, far[0], opposite(*relay, "y"), far[1]
    return project(place, (over_h, over_hk), far_weight, total)


def solution(mesh):
    fine = Mesh(mesh.devices.reshape(4, 4, 4, 2, 2), ("y", "z", "x", "h", "k"))
    chan = ("h", "k")
    return jax.shard_map(
        local,
        mesh=fine,
        in_specs=(
            P(SEQ, chan),
            P(SEQ, chan),
            P(SEQ, chan),
            P(None, SEQ, None, chan),
            P(chan),
            P(chan + SEQ, None),
        ),
        out_specs=P(SEQ, chan),
        check_vma=False,
    )
```

```python
import functools

import numpy as np

import jax
import jax.numpy as jnp
import ml_dtypes
from jax import lax
from jax.experimental import pallas as pl
from jax.experimental.pallas import tpu as pltpu
from jax.sharding import Mesh, PartitionSpec as P

BF, F32 = jnp.bfloat16, jnp.float32
SEQ = ("y", "z", "x")
TOK, NSEQ, CLASSES = 256, 64, 128
FULL = CLASSES * TOK
BIG = 56 << 20
SMALL = 16 << 20
KEPT = 72
GATE = 512


def split(table):
    hi = table.astype(ml_dtypes.bfloat16)
    lo = (table - hi.astype(np.float64)).astype(ml_dtypes.bfloat16)
    return hi, lo


def tables():
    classes = np.concatenate([np.arange(0, CLASSES, 2), np.arange(1, CLASSES, 2)])
    blocks, rows = np.arange(NSEQ), np.arange(TOK)
    kept = np.arange(KEPT)
    real = (kept <= CLASSES // 2)[:, None]
    same = (kept[:, None] == classes[None, :]) & real
    other = (CLASSES - kept[:, None] == classes[None, :]) & real & ~same
    fold = np.stack([1.0 * same + other, 1.0 * same - other]).astype(ml_dtypes.bfloat16)
    turn = 2 * np.pi * (kept[:, None] * blocks[None, :] % CLASSES) / CLASSES
    cos, sin = np.cos(turn) * real, np.sin(turn) * real
    fwd_hi, fwd_lo = split(np.concatenate([cos, -sin], 0))
    first = np.concatenate([fwd_hi, fwd_lo], 1)
    last = np.concatenate(split(np.concatenate([cos.T, -sin.T], 1) / FULL), 0)
    turn = 2 * np.pi * (rows[:, None] * rows[None, :] % TOK) / TOK
    row_hi, row_lo = split(np.concatenate([np.cos(turn), np.sin(turn)], 0))
    row = np.concatenate([row_hi, row_hi, row_lo], 0)
    turn = 2 * np.pi * (kept[:, None] * rows[None, :]) / FULL
    return fold, first, last, row, np.stack([np.cos(turn), np.sin(turn)]).astype(np.float32)


def dot(a, b):
    return lax.dot_general(a, b, (((1,), (0,)), ((), ())), preferred_element_type=F32)


def parts(value):
    hi = value.astype(BF)
    return hi, (value - hi.astype(F32)).astype(BF)


def prep_kernel(turned_ref, k_ref, v_ref, s_ref, o_ref):
    conv = k_ref[...].astype(F32) * v_ref[...].astype(F32)
    o_ref[:, :TOK] = conv.T.astype(BF)
    row = lax.broadcasted_iota(jnp.int32, (TOK, TOK), 0)
    col = lax.broadcasted_iota(jnp.int32, (TOK, TOK), 1)
    for e in range(2):
        place = jnp.where(turned_ref[e] == 1, TOK - 1 - row, row)
        order = jnp.where(place == col, 1.0, 0.0).astype(BF)
        for j in (e, 2 + e):
            o_ref[:, TOK * (j + 1) : TOK * (j + 2)] = dot(s_ref[j].T.astype(BF), order).astype(BF)


def prep(turned, key, value, spectra):
    width = key.shape[1]
    blk = 512
    tok = pl.BlockSpec((TOK, blk), lambda i, turned: (0, i))
    return pl.pallas_call(
        prep_kernel,
        grid_spec=pltpu.PrefetchScalarGridSpec(
            num_scalar_prefetch=1,
            grid=(width // blk,),
            in_specs=[tok, tok, pl.BlockSpec((4, TOK, blk), lambda i, turned: (0, 0, i))],
            out_specs=pl.BlockSpec((blk, 5 * TOK), lambda i, turned: (i, 0)),
        ),
        out_shape=jax.ShapeDtypeStruct((width, 5 * TOK), BF),
        compiler_params=pltpu.CompilerParams(vmem_limit_bytes=BIG),
        name="prep",
    )(turned, key, value, spectra)


GROUP = 8


def widen(src, dst, columns, base):
    def chunk(i, _):
        rows = pl.ds(pl.multiple_of(i * 64, 64), 64)
        for c in range(columns):
            dst[base + c, rows, :] = src[rows, c * 128 : c * 128 + 128].astype(F32)
        return 0

    lax.fori_loop(0, src.shape[0] // 64, chunk, 0)


def rows_of(ref, h, chans, col):
    rows = pl.ds(h, NSEQ, stride=chans)
    return jnp.concatenate([ref[2 * col, rows, :], ref[2 * col + 1, rows, :]], 1)


def row_section(stacked, row_ref):
    hi = jnp.concatenate([piece for pieces in stacked[0::2] for piece in pieces], 0)
    lo = jnp.concatenate([piece for pieces in stacked[1::2] for piece in pieces], 0)
    return dot(jnp.concatenate([hi, lo, hi], 1), row_ref[...])


def fetch(pairs, sems):
    copies = [pltpu.make_async_copy(src, dst, sems.at[i]) for i, (src, dst) in enumerate(pairs)]
    for copy in copies:
        copy.start()
    return copies


def convolve_kernel(r_any, fold_any, first_any, last_any, row_any, turn_any, o_ref, rx, rs, xs, ys, freq, fold_ref, first_ref, last_ref, row_ref, turn_ref, sems):
    chans = rx.shape[0] // NSEQ
    copies = fetch(
        [
            (r_any.at[:, pl.ds(0, TOK)], rx),
            (first_any, first_ref),
            (turn_any, turn_ref),
            (row_any, row_ref),
            (r_any.at[:, pl.ds(TOK, 4 * TOK)], rs),
            (fold_any, fold_ref),
            (last_any, last_ref),
        ],
        sems,
    )
    copies[0].wait()
    widen(rx, xs, 2, 0)
    for copy in copies[1:4]:
        copy.wait()

    def response(h, part):
        pair = [rows_of(xs, h, chans, 1 + 2 * part + e).astype(BF) for e in range(2)]
        return dot(fold_ref[part], jnp.concatenate(pair, 0))

    def ahead(g, _):
        tc, ts = turn_ref[0], turn_ref[1]
        stacked = []
        for j in range(GROUP):
            x = rows_of(xs, g * GROUP + j, chans, 0).astype(BF)
            a = dot(first_ref[...], jnp.concatenate([x, x], 0))
            ar, ai = a[:KEPT], a[KEPT:]
            ar, ai = parts(ar * tc + ai * ts), parts(ai * tc - ar * ts)
            stacked += [[jnp.concatenate([ar[n], ai[n]], 1), jnp.concatenate([ai[n], -ar[n]], 1)] for n in (0, 1)]
        size = GROUP * 2 * KEPT
        freq[pl.ds(pl.multiple_of(g * size, size), size), :] = row_section(stacked, row_ref)
        return 0

    lax.fori_loop(0, chans // GROUP, ahead, 0)
    for copy in copies[4:]:
        copy.wait()
    widen(rs, xs, 8, 2)

    def back(g, _):
        tc, ts = turn_ref[0], turn_ref[1]
        stacked = []
        for j in range(GROUP):
            h = g * GROUP + j
            rr, ri = response(h, 0), response(h, 1)
            base = pl.multiple_of(h * 2 * KEPT, 8)
            xr, xi = freq[pl.ds(base, KEPT), :], freq[pl.ds(base + KEPT, KEPT), :]
            pr, pi = parts(rr * xr - ri * xi), parts(rr * xi + ri * xr)
            stacked += [[jnp.concatenate([pr[n], -pi[n]], 1), jnp.concatenate([pi[n], pr[n]], 1)] for n in (0, 1)]
        rows = row_section(stacked, row_ref)
        for j in range(GROUP):
            h = g * GROUP + j
            base = 2 * KEPT * j
            br, bi = rows[base : base + KEPT], rows[base + KEPT : base + 2 * KEPT]
            hi, lo = parts(jnp.concatenate([br * tc - bi * ts, bi * tc + br * ts], 0))
            both = dot(last_ref[...], hi)
            y = both[:NSEQ] + both[NSEQ:] + dot(last_ref[:NSEQ], lo)
            for c in range(2):
                ys[c, pl.ds(h, NSEQ, stride=chans), :] = y[:, c * 128 : c * 128 + 128]
        return 0

    lax.fori_loop(0, chans // GROUP, back, 0)
    for c in range(2):
        o_ref[:, c * 128 : c * 128 + 128] = ys[c].astype(BF)


VMEM = pl.BlockSpec(memory_space=pltpu.VMEM)
ANY = pl.BlockSpec(memory_space=pl.ANY)


def constants():
    return [jnp.asarray(table) for table in tables()]


def held(consts):
    return [pltpu.VMEM(c.shape, c.dtype) for c in consts]


def block(shape):
    return pl.BlockSpec(shape, lambda i: (0,) * len(shape))


def convolve(received):
    rows = received.shape[0]
    consts = constants()
    return pl.pallas_call(
        convolve_kernel,
        grid=(1,),
        in_specs=[ANY] * (1 + len(consts)),
        out_specs=block((rows, TOK)),
        out_shape=jax.ShapeDtypeStruct((rows, TOK), BF),
        scratch_shapes=[
            pltpu.VMEM((rows, TOK), BF),
            pltpu.VMEM((rows, 4 * TOK), BF),
            pltpu.VMEM((10, rows, 128), F32),
            pltpu.VMEM((2, rows, 128), F32),
            pltpu.VMEM((rows // NSEQ * 2 * KEPT, TOK), F32),
        ]
        + held(consts)
        + [pltpu.SemaphoreType.DMA((2 + len(consts),))],
        compiler_params=pltpu.CompilerParams(vmem_limit_bytes=BIG),
        cost_estimate=pl.CostEstimate(flops=16 << 30, bytes_accessed=4 << 20, transcendentals=0),
        name="convolve",
    )(received, *consts)


def gate_kernel(y_ref, q_ref, k_ref, v_ref, s_ref, o_ref):
    conv = k_ref[...].astype(F32) * v_ref[...].astype(F32)
    direct = (s_ref[...] * conv).T
    o_ref[...] = (q_ref[...].astype(F32).T * (y_ref[...].astype(F32) + direct)).astype(BF)


def gate(y, query, key, value, gain):
    width = y.shape[0]
    blk = GATE
    tok = pl.BlockSpec((TOK, blk), lambda i: (0, i))
    chan = pl.BlockSpec((blk, TOK), lambda i: (i, 0))
    return pl.pallas_call(
        gate_kernel,
        grid=(width // blk,),
        in_specs=[chan, tok, tok, tok, pl.BlockSpec((1, blk), lambda i: (0, i))],
        out_specs=chan,
        out_shape=jax.ShapeDtypeStruct((width, TOK), BF),
        compiler_params=pltpu.CompilerParams(vmem_limit_bytes=SMALL),
        name="gate",
    )(y, query, key, value, gain)


def sum_terms(g_refs, w_refs, total):
    own, left, opp0, opp1, right = w_refs
    for d, pair in enumerate(((own, own), (left, left), (opp0, opp1), (right, right))):
        terms = []
        for c, (g_ref, w_ref) in enumerate(zip(g_refs, pair)):
            w = w_ref[...] if d == 2 else w_ref[c]
            terms.append(dot(w.reshape(256, w.shape[-1]), g_ref[...]))
        total[d * 256 : d * 256 + 256, :] = terms[0] + terms[1]


def near_kernel(g0, g1, own, left, opp0, opp1, right, o_ref):
    sum_terms((g0, g1), (own, left, opp0, opp1, right), o_ref)


def far_kernel(place_ref, g0, g1, own, left, opp0, opp1, right, near_ref, o_ref, total):
    sum_terms((g0, g1), (own, left, opp0, opp1, right), total)

    def line(ref, a, b, c):
        return ref[pl.ds(pl.multiple_of(((a * 4 + b) * 4 + c) * 16, 16), 16), :]

    for y in range(4):
        dy, pieces = (place_ref[0] - y) & 3, []
        for z in range(4):
            for x in range(4):
                dz, dx = (place_ref[1] - z) & 3, (place_ref[2] - x) & 3
                pieces.append(line(near_ref, dx, dy, dz) + line(total, dy, dx, dz))
        o_ref[:, y * 256 : y * 256 + 256] = jnp.concatenate(pieces, 0).T.astype(BF)


def project(place, pieces, weights, near=None):
    own, left, (opp0, opp1), right = weights
    args = [*pieces, own, left, opp0, opp1, right] + ([] if near is None else [near])

    def whole(shape):
        return pl.BlockSpec(shape, lambda i, *_: (0,) * len(shape))

    shape, kind = ((1024, TOK), F32) if near is None else ((TOK, 1024), BF)
    return pl.pallas_call(
        near_kernel if near is None else far_kernel,
        grid_spec=pltpu.PrefetchScalarGridSpec(
            num_scalar_prefetch=0 if near is None else 1,
            grid=(1,),
            in_specs=[whole(a.shape) for a in args],
            out_specs=whole(shape),
            scratch_shapes=[] if near is None else [pltpu.VMEM((1024, TOK), F32)],
        ),
        out_shape=jax.ShapeDtypeStruct(shape, kind),
        compiler_params=pltpu.CompilerParams(vmem_limit_bytes=24 << 20),
        cost_estimate=pl.CostEstimate(flops=1 << 35, bytes_accessed=6 << 20, transcendentals=0),
        name="near" if near is None else "far",
    )(*([] if near is None else [place]), *args)


def ring(axis, step):
    return axis, [(a, (a + step) % 4) for a in range(4)]


def beside(piece, axis):
    return lax.ppermute(piece, *ring(axis, 1)), lax.ppermute(piece, *ring(axis, -1))


def opposite(left, right, axis):
    return lax.ppermute(left, *ring(axis, 1)), lax.ppermute(right, *ring(axis, -1))


def around(piece, axis):
    left, right = beside(piece, axis)
    return piece, left, opposite(left[0], right[1], axis), right


def stacked(pieces):
    own, left, (opp0, opp1), right = pieces
    return jnp.stack([jnp.stack([own[c], left[c], opp, right[c]]) for c, opp in enumerate((opp0, opp1))])


def gather_weight(weight, chan, after):
    pieces = [weight] + [
        lax.ppermute(weight, "z", [(a, (a + d) % 4) for a in range(4)]) for d in (1, 2, 3)
    ]
    *pieces, after = lax.optimization_barrier((*pieces, after))
    width = weight.shape[1] // 4
    rows = jnp.stack(pieces)
    near, far = [
        jnp.stack([lax.dynamic_slice_in_dim(rows, (chan ^ j) * width, width, 2) for j in pair])
        for pair in ((0, 1), (2, 3))
    ]
    far = stacked(around(far, "x"))
    near = stacked(around(near, "y"))
    return (near, *beside(near, "x")), (far, *beside(far, "y")), after


def exchange(send):
    send = send.reshape(NSEQ, -1, send.shape[1])
    got = lax.all_to_all(send, SEQ, split_axis=0, concat_axis=0, tiled=True)
    return got.reshape(-1, got.shape[2])


def local(query, key, value, spectra, gain, weight):
    swap = [(0, 1), (1, 0)]
    index = (lax.axis_index("y") * 4 + lax.axis_index("z")) * 4 + lax.axis_index("x")
    turned = (2 * index + jnp.arange(2) > CLASSES // 2).astype(jnp.int32)
    send = prep(turned, key, value, spectra.reshape((4,) + spectra.shape[2:]))
    h, k = lax.axis_index("h"), lax.axis_index("k")
    (near_own, *near), (far_own, *far), send = gather_weight(weight, h * 2 + k, send)
    send, query, key, value, gain = lax.optimization_barrier((send, query, key, value, gain))
    got = exchange(send)
    y = convolve(got)
    y, near, far = lax.optimization_barrier((y, near, far))
    y = exchange(y)
    opposites = opposite(near[0][0], near[1][1], "x")
    relay = far[0][0], far[1][1]
    y, relay = lax.optimization_barrier((y, relay))
    gated = gate(y, query, key, value, gain[None, :])
    over_k = lax.ppermute(gated, "k", swap)
    over_h = lax.ppermute(gated, "h", swap)
    over_k, relay, opposites = lax.optimization_barrier((over_k, relay, opposites))
    near_weight = near_own, near[0], opposites, near[1]
    place = jnp.stack([lax.axis_index(axis) for axis in ("y", "z", "x")]).astype(jnp.int32)
    total = project(place, (gated, over_k), near_weight)
    over_h, total = lax.optimization_barrier((over_h, total))
    over_hk = lax.ppermute(over_h, "k", swap)
    far_weight = far_own, far[0], opposite(*relay, "y"), far[1]
    return project(place, (over_h, over_hk), far_weight, total)


def solution(mesh):
    fine = Mesh(mesh.devices.reshape(4, 4, 4, 2, 2), ("y", "z", "x", "h", "k"))
    chan = ("h", "k")
    return jax.shard_map(
        local,
        mesh=fine,
        in_specs=(
            P(SEQ, chan),
            P(SEQ, chan),
            P(SEQ, chan),
            P(None, SEQ, None, chan),
            P(chan),
            P(chan + SEQ, None),
        ),
        out_specs=P(SEQ, chan),
        check_vma=False,
    )
```
